256 devices in a mesh: frame: 8 (over z_hi, core), slab: 32 (over z_lo, x, y).
Axes of the slice: x: 4, y: 4, z: 8 (z_hi: 4, z_lo: 2; z = z_hi * 2 + z_lo), core: 2. Of those that a mesh axis runs over, the one named last changes fastest.
Arguments:
- volume: float32 [8, 1024, 16384], P('frame', 'slab'), may hold values from -6 to 6
- measured: float32 [8, 2, 1024, 16384], P('frame', None, None, 'slab'), may hold values from -6 to 6
- cutoff: int32 [8, 16384], P('frame', 'slab'), may hold values from 128 to 384
Outputs:
- smoothed: float32 [8, 1024, 16384], P('frame', 'slab')
The draws below stay inside these ranges and needn't reach their ends.
All inputs are finite; a program needn't handle non-finite values.
Results may differ from the reference program's by a relative error of at most 0.0003.
Values sent between devices are 32-bit elements; how exact they have to be, the bound alone decides.
A program may use at most 128 MiB of HBM per device.

```python
import jax
import jax.numpy as jnp
from jax import lax

NZ = 1024
PIX = 16384
FRAMES = 8


def set_ends(array, stream_key, smallest, high):
    place = [jax.random.randint(jax.random.fold_in(stream_key, axis), (), 0, length) for axis, length in enumerate(array.shape)]
    longest = array.shape.index(max(array.shape))
    beside = place[:longest] + [(place[longest] + 1) % array.shape[longest]] + place[longest + 1:]
    return array.at[tuple(place)].set(smallest).at[tuple(beside)].set(high)


def shard_levels(stream_key, extent, cuts, low, largest):
    gain = 1.0
    for position, shards_of in cuts:
        heights = jax.random.uniform(jax.random.fold_in(jax.random.fold_in(stream_key, 6), position), (shards_of,), jnp.float32, low / len(cuts), largest / len(cuts))
        gain = gain * jnp.repeat(jnp.exp(heights), extent[position] // shards_of).reshape((-1,) + (1,) * (len(extent) - 1 - position))
    return gain


def scatter_about(stream_key, extent, spread, limit, split=(), held_as=jnp.bfloat16):
    values = jax.random.normal(stream_key, extent, jnp.float32) * spread
    if len(split) > 0:
        values = shard_levels(stream_key, extent, split, -0.22, 0.18) * values
    return jnp.clip(values, min=-limit, max=limit).astype(held_as)


def setup_inputs(seed: int = 0) -> dict:
    streams_of = jax.random.split(jax.random.key(seed), 4)
    volume = scatter_about(streams_of[0], (FRAMES, NZ, PIX), 1.0, 6.0, ((0, 8), (1, 32)), jnp.float32)
    measured = scatter_about(streams_of[1], (FRAMES, 2, NZ, PIX), 1.0, 6.0, ((0, 8), (3, 32)), jnp.float32)
    cutoff = set_ends(jax.random.randint(streams_of[2], (FRAMES, PIX), NZ // 8, 3 * NZ // 8 + 1), jax.random.fold_in(streams_of[2], 1), NZ // 8, (3 * NZ // 8 + 1) - 1).astype(jnp.int32)
    return dict(volume=volume, measured=measured, cutoff=cutoff)


tv_step_size = 0.25
tv_weight = 1.0

def tv_step(extended, anchor, first_frame, frames):
    difference = extended[1:] - extended[:-1]
    frame_ids = first_frame + jnp.arange(difference.shape[0], dtype=jnp.int32)
    inside = ((frame_ids >= 0) & (frame_ids <= frames - 2))[:, None, None]
    fluxes = jnp.where(inside, difference / jnp.sqrt(difference * difference + 1.0), 0.0)
    interior = extended[1:-1]
    return interior - tv_step_size * (interior - anchor + tv_weight * (fluxes[:-1] - fluxes[1:]))

def transform_frame(packed):
    column_field, spectrum, limits = packed
    scale = jnp.sqrt(jnp.float32(NZ))
    forward = jnp.fft.fft(column_field, axis=0)
    real_part = jnp.real(forward) / scale
    imag_part = jnp.imag(forward) / scale
    indices = jnp.arange(NZ, dtype=jnp.int32)
    signed = jnp.where(indices < NZ // 2, indices, indices - NZ)
    measured_mask = jnp.abs(signed)[:, None] <= limits[None, :]
    real_part = jnp.where(measured_mask, spectrum[0], real_part)
    imag_part = jnp.where(measured_mask, spectrum[1], imag_part)
    backward = jnp.fft.ifft(lax.complex(real_part, imag_part), axis=0)
    return jnp.real(backward) * scale

def reference(volume, measured, cutoff):
    anchor = lax.map(transform_frame, (volume, measured, cutoff))
    current = anchor
    for step in range(2):
        extended = jnp.pad(current, ((1, 1), (0, 0), (0, 0)))
        current = tv_step(extended, anchor, -1, FRAMES)
    return current
```

```python
import functools

import jax
import jax.numpy as jnp
import ml_dtypes
import numpy as np
from jax import lax
from jax.experimental import pallas as pl
from jax.experimental.pallas import tpu as pltpu
from jax.sharding import PartitionSpec as P

MESH = pl.DeviceIdType.MESH
F32, BF16 = jnp.float32, jnp.bfloat16
step_size = 0.25
tv_weight = 1.0


def tables(length):
    index = np.arange(length, dtype=np.int64)
    angle = (index[:, None] * index[None, :] % length) * (2.0 * np.pi / length)
    parts = []
    for table in (np.cos(angle), -np.sin(angle)):
        table = table / np.sqrt(length)
        head = table.astype(ml_dtypes.bfloat16)
        rest = (table - head.astype(np.float64)).astype(ml_dtypes.bfloat16)
        parts += [head, rest]
    return parts


def flux(d):
    return d * lax.rsqrt(d * d + 1.0)


def split(x):
    head = x.astype(BF16)
    rest = (x - head.astype(F32)).astype(BF16)
    return head, rest


def kernel(
    cfg,
    volume, measured, cutoff, ch_hbm, cl_hbm, sh_hbm, sl_hbm,
    out,
    cols, anchor_cols, meas, ch, cl, sh, sl, rhs, rhs2,
    slab, halo, part, own1, near1, part1,
    local_sem, meas_sem, f_send, f_recv, b_send, b_recv, h_send, h_recv, p_send, p_recv, q_send, q_recv,
):
    length, slabs, rows, width, n, chunks, kr, kp, kranges = cfg
    half = slabs // 2
    frame, me = lax.axis_index("frame"), lax.axis_index("slab")
    frames = lax.axis_size("frame")
    block, core = lax.div(frame, 2), lax.rem(frame, 2)
    blocks = frames // 2
    z_lo, place = lax.div(me, half), lax.rem(me, half)
    partner = frame + 1 - 2 * core
    full_frame = jnp.where(z_lo == 1, 2 * block + 2, 2 * block - 1)
    full_there = jnp.where(z_lo == 1, block < blocks - 1, block > 0)
    half_frame = jnp.where(z_lo == 1, 2 * block - 1, 2 * block + 2)
    half_there = jnp.where(z_lo == 1, block > 0, block < blocks - 1)
    near_block = jnp.where(core == 0, block - 1, block + 1)
    near_there = jnp.where(core == 0, block > 0, block < blocks - 1)

    def send(src, dst, send_sem, recv_sem, to_frame, to_slab):
        pltpu.make_async_remote_copy(
            src_ref=src, dst_ref=dst, send_sem=send_sem, recv_sem=recv_sem,
            device_id=(to_frame, to_slab), device_id_type=MESH,
        ).start()

    def wait(like, sem):
        pltpu.make_async_copy(like, like, sem).wait()

    def peer_of(step, across):
        if half == 16:
            there = lax.rem(lax.div(place, 4) + lax.div(step, 4), 4) * 4 + lax.rem(place + step, 4)
        else:
            there = lax.rem(place + step, half)
        return (1 - z_lo if across else z_lo) * half + there

    local = [
        pltpu.make_async_copy(src, dst, local_sem.at[i])
        for i, (src, dst) in enumerate(((ch_hbm, ch), (cl_hbm, cl), (sh_hbm, sh), (sl_hbm, sl)))
    ]
    local += [
        pltpu.make_async_copy(measured.at[0, :, :, pl.ds(c * n, n)], meas.at[c], meas_sem.at[c])
        for c in range(chunks)
    ]
    for copy in local:
        copy.start()

    barrier = pltpu.get_barrier_semaphore()

    def greet(to_frame, to_slab):
        pl.semaphore_signal(barrier, inc=1, device_id=(to_frame, to_slab), device_id_type=MESH)

    @pl.loop(0, half)
    def _(step):
        greet(frame, peer_of(step, True))

        @pl.when(step > 0)
        def _():
            greet(frame, peer_of(step, False))

        @pl.when(near_there & (z_lo == core))
        def _():
            greet(2 * near_block, peer_of(step, True))
            greet(2 * near_block + 1, peer_of(step, True))

    greet(partner, me)

    @pl.when(near_there)
    def _():
        greet(2 * near_block, me)
        greet(2 * near_block + 1, me)

    expected = (
        slabs
        + jnp.where(full_there, half + 1, 0)
        + jnp.where(half_there, 1, 0)
    )
    pl.semaphore_wait(barrier, expected)

    @pl.loop(0, chunks)
    def _(c):
        def source(peer):
            return volume.at[0, :, pl.ds(pl.multiple_of(peer * width + c * n, n), n)]

        target = cols.at[c, pl.ds(pl.multiple_of(me * rows, rows), rows), :]

        @pl.loop(0, half)
        def _(step):
            peer = peer_of(step, True)
            send(source(peer), target, f_send.at[c], f_recv.at[c], frame, peer)

            @pl.when(step > 0)
            def _():
                peer = peer_of(step, False)
                send(source(peer), target, f_send.at[c], f_recv.at[c], frame, peer)

        pltpu.make_async_copy(source(me), target, f_recv.at[c]).start()

    for copy in local[:4]:
        copy.wait()

    if kp > kr:
        rhs2[:, kr:, :] = jnp.zeros((2, kp - kr, 2 * n), BF16)
    tile = min(256, length)
    tiles = length // tile

    def product(at, ranges, right):
        wide, narrow = None, None
        for half_index, (head, rest) in enumerate(((ch, cl), (sh, sl))):
            for low, high, base in ranges:
                both = right[half_index, base : base + high - low, :]
                first = jnp.dot(head[at, low:high], both, preferred_element_type=F32)
                second = jnp.dot(rest[at, low:high], both[:, :n], preferred_element_type=F32)
                wide = first if wide is None else wide + first
                narrow = second if narrow is None else narrow + second
        return wide[:, :n] + wide[:, n:] + narrow

    def transform(c):
        limit = cutoff[0:1, pl.ds(pl.multiple_of(c * n, n), n)]
        wait(meas.at[c], meas_sem.at[c])
        for low, high, base in kranges:
            k = lax.broadcasted_iota(jnp.int32, (high - low, n), 0) + low
            inside = jnp.minimum(k, length - k) <= limit
            for i in range(2):
                head, rest = split(jnp.where(inside, meas[c, i, low:high, :], 0.0))
                rhs[i, base : base + high - low, :n] = head
                rhs[i, base : base + high - low, n:] = rest

        @pl.loop(0, tiles)
        def _(t):
            at = pl.ds(pl.multiple_of(t * tile, tile), tile)
            anchor_cols[c, at, :] = product(at, kranges, rhs)

        wait(cols.at[c], f_recv.at[c])
        head, rest = split(cols[c])
        rhs[0, 0:length, :n] = head
        rhs[0, 0:length, n:] = rest
        k = lax.broadcasted_iota(jnp.int32, (kr, n), 0)
        weight = jnp.where(k <= limit, jnp.where(k == 0, 1.0, 2.0), 0.0)
        for i, (head, rest) in enumerate(((ch, cl), (sh, sl))):
            both = rhs[0, 0:length, :]
            wide = jnp.dot(head[:kr, :], both, preferred_element_type=F32)
            narrow = jnp.dot(rest[:kr, :], both[:, :n], preferred_element_type=F32)
            first, second = split((wide[:, :n] + wide[:, n:] + narrow) * weight)
            rhs2[i, :kr, :n] = first
            rhs2[i, :kr, n:] = second

        @pl.loop(0, tiles)
        def _(t):
            at = pl.ds(pl.multiple_of(t * tile, tile), tile)
            anchor_cols[c, at, :] = anchor_cols[c, at, :] + cols[c, at, :] - product(at, ((0, kp, 0),), rhs2)

    def send_back(c):
        def source(peer):
            return anchor_cols.at[c, pl.ds(pl.multiple_of(peer * rows, rows), rows), :]

        @pl.loop(0, half)
        def _(step):
            peer = peer_of(step, True)
            send(source(peer), slab.at[c, me], b_send.at[c], b_recv.at[c], frame, peer)

            @pl.when(step > 0)
            def _():
                peer = peer_of(step, False)
                send(source(peer), slab.at[c, me], b_send.at[c], b_recv.at[c], frame, peer)

        pltpu.make_async_copy(source(me), slab.at[c, me], b_recv.at[c]).start()

        @pl.when(full_there)
        def _():
            @pl.loop(0, half)
            def _(step):
                peer = peer_of(step, True)
                send(source(peer), halo.at[c, core, me], h_send.at[c], h_recv.at[c], full_frame, peer)

    def send_halo(c):
        wait(slab.at[c], b_recv.at[c])

        @pl.when(full_there)
        def _():
            send(slab.at[c], halo.at[c, core], h_send.at[c], h_recv.at[c], full_frame, me)

        @pl.when(half_there)
        def _():
            some = pl.ds(z_lo * half, half)
            send(slab.at[c, some], halo.at[c, core, some], h_send.at[c], h_recv.at[c], half_frame, me)

        send(slab.at[c], part.at[c], p_send.at[c], p_recv.at[c], partner, me)

    @pl.loop(0, chunks)
    def _(c):
        transform(c)
        send_back(c)

        @pl.when(c > 0)
        def _():
            send_halo(c - 1)

    send_halo(chunks - 1)

    near, far = 1 - core, core

    def first_step(c):
        wait(part.at[c], p_recv.at[c])

        @pl.when(near_there)
        def _():
            wait(halo.at[c], h_recv.at[c])

        @pl.loop(0, slabs)
        def _(b):
            a, p = slab[c, b], part[c, b]
            x, y = halo[c, near, b], halo[c, far, b]
            across = jnp.where(near_there, flux(x - a), 0.0)
            own1[c, b] = a + step_size * tv_weight * (flux(p - a) + across)
            near1[c, b] = x + step_size * tv_weight * (flux(y - x) - across)

        send(own1.at[c], part1.at[c], q_send.at[c], q_recv.at[c], partner, me)

    def second_step(c):
        wait(part1.at[c], q_recv.at[c])

        @pl.loop(0, slabs)
        def _(b):
            a, u = slab[c, b], own1[c, b]
            across = jnp.where(near_there, flux(near1[c, b] - u), 0.0)
            result = u - step_size * ((u - a) - tv_weight * (flux(part1[c, b] - u) + across))
            out[0, :, pl.ds(pl.multiple_of(b * width + c * n, n), n)] = result

    @pl.loop(0, chunks)
    def _(c):
        first_step(c)

        @pl.when(c > 0)
        def _():
            second_step(c - 1)

    second_step(chunks - 1)

    @pl.loop(0, chunks)
    def _(c):
        wait(slab.at[c, pl.ds(0, slabs - 1)], f_send.at[c])
        wait(slab.at[c, pl.ds(0, slabs - 1)], b_send.at[c])
        wait(slab.at[c], p_send.at[c])
        wait(slab.at[c], q_send.at[c])

        @pl.when(full_there)
        def _():
            wait(slab.at[c], h_send.at[c])
            wait(slab.at[c, pl.ds(0, half)], h_send.at[c])

        @pl.when(half_there)
        def _():
            wait(slab.at[c, pl.ds(0, half)], h_send.at[c])


def on_device(volume, measured, cutoff):
    _, rows, pixels = volume.shape
    _, _, length, width = measured.shape
    slabs = pixels // width
    n = 128
    chunks = width // n
    most = 3 * length // 8
    kp = length // 2
    kr = -(-(most + 1) // 16) * 16
    upper = (length - most) // 128 * 128
    kranges = ((0, kp, 0), (upper, length, kp)) if upper >= kp else ((0, length, 0),)
    cfg = (length, slabs, rows, width, n, chunks, kr, kp, kranges)
    piece = (chunks, slabs, rows, n)
    dma = pltpu.SemaphoreType.DMA
    hbm = pl.BlockSpec(memory_space=pl.ANY)
    vmem = pl.BlockSpec(memory_space=pltpu.VMEM)
    return pl.pallas_call(
        functools.partial(kernel, cfg),
        out_shape=jax.ShapeDtypeStruct(volume.shape, F32),
        in_specs=[hbm, hbm, vmem, hbm, hbm, hbm, hbm],
        out_specs=vmem,
        scratch_shapes=[
            pltpu.VMEM((chunks, length, n), F32),
            pltpu.VMEM((chunks, length, n), F32),
            pltpu.VMEM((chunks, 2, length, n), F32),
            *[pltpu.VMEM((length, length), BF16)] * 4,
            pltpu.VMEM((2, length, 2 * n), BF16),
            pltpu.VMEM((2, kp, 2 * n), BF16),
            pltpu.VMEM(piece, F32),
            pltpu.VMEM((chunks, 2, slabs, rows, n), F32),
            *[pltpu.VMEM(piece, F32)] * 4,
            dma((4,)),
            *[dma((chunks,))] * 11,
        ],
        compiler_params=pltpu.CompilerParams(
            collective_id=0, has_side_effects=True, vmem_limit_bytes=60 * 1024 * 1024
        ),
        cost_estimate=pl.CostEstimate(flops=10**10, bytes_accessed=2**24, transcendentals=0),
    )(volume, measured, cutoff, *tables(length))


def solution(mesh):
    placed = (P("frame", "slab", None), P("frame", None, None, "slab"), P("frame", "slab"))
    return jax.shard_map(
        on_device, mesh=mesh, in_specs=placed, out_specs=P("frame", "slab", None), check_vma=False
    )
```

```python
import functools

import jax
import jax.numpy as jnp
import ml_dtypes
import numpy as np
from jax import lax
from jax.experimental import pallas as pl
from jax.experimental.pallas import tpu as pltpu
from jax.sharding import PartitionSpec as P

MESH = pl.DeviceIdType.MESH
F32, BF16 = jnp.float32, jnp.bfloat16
step_size = 0.25
tv_weight = 1.0


def tables(length):
    index = np.arange(length, dtype=np.int64)
    angle = (index[:, None] * index[None, :] % length) * (2.0 * np.pi / length)
    parts = []
    for table in (np.cos(angle), -np.sin(angle)):
        table = table / np.sqrt(length)
        head = table.astype(ml_dtypes.bfloat16)
        rest = (table - head.astype(np.float64)).astype(ml_dtypes.bfloat16)
        parts += [head, rest]
    return parts


def flux(d):
    return d * lax.rsqrt(d * d + 1.0)


def split(x):
    head = x.astype(BF16)
    rest = (x - head.astype(F32)).astype(BF16)
    return head, rest


def kernel(
    cfg,
    volume, measured, cutoff, ch_hbm, cl_hbm, sh_hbm, sl_hbm,
    out,
    cols, anchor_cols, meas, ch, cl, sh, sl, rhs, rhs2,
    slab, halo, part, own1, near1, part1,
    local_sem, meas_sem, f_send, f_recv, b_send, b_recv, h_send, h_recv, p_send, p_recv, q_send, q_recv,
):
    length, slabs, rows, width, n, chunks, kr, kp, kranges = cfg
    half = slabs // 2
    ahead = min(2, chunks)
    frame, me = lax.axis_index("frame"), lax.axis_index("slab")
    frames = lax.axis_size("frame")
    block, core = lax.div(frame, 2), lax.rem(frame, 2)
    blocks = frames // 2
    z_lo, place = lax.div(me, half), lax.rem(me, half)
    partner = frame + 1 - 2 * core
    full_frame = jnp.where(z_lo == 1, 2 * block + 2, 2 * block - 1)
    full_there = jnp.where(z_lo == 1, block < blocks - 1, block > 0)
    half_frame = jnp.where(z_lo == 1, 2 * block - 1, 2 * block + 2)
    half_there = jnp.where(z_lo == 1, block > 0, block < blocks - 1)
    near_block = jnp.where(core == 0, block - 1, block + 1)
    near_there = jnp.where(core == 0, block > 0, block < blocks - 1)

    def send(src, dst, send_sem, recv_sem, to_frame, to_slab):
        pltpu.make_async_remote_copy(
            src_ref=src, dst_ref=dst, send_sem=send_sem, recv_sem=recv_sem,
            device_id=(to_frame, to_slab), device_id_type=MESH,
        ).start()

    def wait(like, sem):
        pltpu.make_async_copy(like, like, sem).wait()

    def peer_of(step, across):
        if half == 16:
            there = lax.rem(lax.div(place, 4) + lax.div(step, 4), 4) * 4 + lax.rem(place + step, 4)
        else:
            there = lax.rem(place + step, half)
        return (1 - z_lo if across else z_lo) * half + there

    local = [
        pltpu.make_async_copy(src, dst, local_sem.at[i])
        for i, (src, dst) in enumerate(((ch_hbm, ch), (cl_hbm, cl), (sh_hbm, sh), (sl_hbm, sl)))
    ]
    local += [
        pltpu.make_async_copy(measured.at[0, :, :, pl.ds(c * n, n)], meas.at[c], meas_sem.at[c])
        for c in range(chunks)
    ]
    for copy in local:
        copy.start()

    barrier = pltpu.get_barrier_semaphore()

    def greet(to_frame, to_slab):
        pl.semaphore_signal(barrier, inc=1, device_id=(to_frame, to_slab), device_id_type=MESH)

    @pl.loop(0, half)
    def _(step):
        greet(frame, peer_of(step, True))

        @pl.when(step > 0)
        def _():
            greet(frame, peer_of(step, False))

        @pl.when(near_there & (z_lo == core))
        def _():
            greet(2 * near_block, peer_of(step, True))
            greet(2 * near_block + 1, peer_of(step, True))

    greet(partner, me)

    @pl.when(near_there)
    def _():
        greet(2 * near_block, me)
        greet(2 * near_block + 1, me)

    expected = (
        slabs
        + jnp.where(full_there, half + 1, 0)
        + jnp.where(half_there, 1, 0)
    )
    pl.semaphore_wait(barrier, expected)

    def send_columns(c):
        def source(peer):
            return volume.at[0, :, pl.ds(pl.multiple_of(peer * width + c * n, n), n)]

        target = cols.at[c, pl.ds(pl.multiple_of(me * rows, rows), rows), :]

        @pl.loop(0, half)
        def _(step):
            peer = peer_of(step, True)
            send(source(peer), target, f_send.at[c], f_recv.at[c], frame, peer)

            @pl.when(step > 0)
            def _():
                peer = peer_of(step, False)
                send(source(peer), target, f_send.at[c], f_recv.at[c], frame, peer)

        pltpu.make_async_copy(source(me), target, f_recv.at[c]).start()

    @pl.loop(0, ahead)
    def _(c):
        send_columns(c)

    for copy in local[:4]:
        copy.wait()

    if kp > kr:
        rhs2[:, kr:, :] = jnp.zeros((2, kp - kr, 2 * n), BF16)
    tile = min(256, length)
    tiles = length // tile

    def product(at, ranges, right):
        wide, narrow = None, None
        for half_index, (head, rest) in enumerate(((ch, cl), (sh, sl))):
            for low, high, base in ranges:
                both = right[half_index, base : base + high - low, :]
                first = jnp.dot(head[at, low:high], both, preferred_element_type=F32)
                second = jnp.dot(rest[at, low:high], both[:, :n], preferred_element_type=F32)
                wide = first if wide is None else wide + first
                narrow = second if narrow is None else narrow + second
        return wide[:, :n] + wide[:, n:] + narrow

    def transform(c):
        limit = cutoff[0:1, pl.ds(pl.multiple_of(c * n, n), n)]
        wait(meas.at[c], meas_sem.at[c])
        for low, high, base in kranges:
            k = lax.broadcasted_iota(jnp.int32, (high - low, n), 0) + low
            inside = jnp.minimum(k, length - k) <= limit
            for i in range(2):
                head, rest = split(jnp.where(inside, meas[c, i, low:high, :], 0.0))
                rhs[i, base : base + high - low, :n] = head
                rhs[i, base : base + high - low, n:] = rest

        @pl.loop(0, tiles)
        def _(t):
            at = pl.ds(pl.multiple_of(t * tile, tile), tile)
            anchor_cols[c, at, :] = product(at, kranges, rhs)

        wait(cols.at[c], f_recv.at[c])

        @pl.when(c + ahead < chunks)
        def _():
            send_columns(c + ahead)

        head, rest = split(cols[c])
        rhs[0, 0:length, :n] = head
        rhs[0, 0:length, n:] = rest
        k = lax.broadcasted_iota(jnp.int32, (kr, n), 0)
        weight = jnp.where(k <= limit, jnp.where(k == 0, 1.0, 2.0), 0.0)
        for i, (head, rest) in enumerate(((ch, cl), (sh, sl))):
            both = rhs[0, 0:length, :]
            wide = jnp.dot(head[:kr, :], both, preferred_element_type=F32)
            narrow = jnp.dot(rest[:kr, :], both[:, :n], preferred_element_type=F32)
            first, second = split((wide[:, :n] + wide[:, n:] + narrow) * weight)
            rhs2[i, :kr, :n] = first
            rhs2[i, :kr, n:] = second

        @pl.loop(0, tiles)
        def _(t):
            at = pl.ds(pl.multiple_of(t * tile, tile), tile)
            anchor_cols[c, at, :] = anchor_cols[c, at, :] + cols[c, at, :] - product(at, ((0, kp, 0),), rhs2)

    def send_back(c):
        def source(peer):
            return anchor_cols.at[c, pl.ds(pl.multiple_of(peer * rows, rows), rows), :]

        @pl.loop(0, half)
        def _(step):
            peer = peer_of(step, True)
            send(source(peer), slab.at[c, me], b_send.at[c], b_recv.at[c], frame, peer)

            @pl.when(step > 0)
            def _():
                peer = peer_of(step, False)
                send(source(peer), slab.at[c, me], b_send.at[c], b_recv.at[c], frame, peer)

        pltpu.make_async_copy(source(me), slab.at[c, me], b_recv.at[c]).start()

        @pl.when(full_there)
        def _():
            @pl.loop(0, half)
            def _(step):
                peer = peer_of(step, True)
                send(source(peer), halo.at[c, core, me], h_send.at[c], h_recv.at[c, z_lo], full_frame, peer)

    def send_halo(c):
        wait(slab.at[c], b_recv.at[c])

        for h in (z_lo, 1 - z_lo):
            some = pl.ds(h * half, half)

            @pl.when(full_there)
            def _():
                send(slab.at[c, some], halo.at[c, core, some], h_send.at[c], h_recv.at[c, h], full_frame, me)

            if h is z_lo:

                @pl.when(half_there)
                def _():
                    send(slab.at[c, some], halo.at[c, core, some], h_send.at[c], h_recv.at[c, h], half_frame, me)

        for h in (1 - core, core):
            some = pl.ds(h * half, half)
            send(slab.at[c, some], part.at[c, some], p_send.at[c], p_recv.at[c, h], partner, me)

    @pl.loop(0, chunks)
    def _(c):
        transform(c)
        send_back(c)

        @pl.when(c > 0)
        def _():
            send_halo(c - 1)

    send_halo(chunks - 1)

    near, far = 1 - core, core

    def first_step(c, h):
        some = pl.ds(h * half, half)
        wait(part.at[c, some], p_recv.at[c, h])

        @pl.when(near_there)
        def _():
            wait(halo.at[c, 0], h_recv.at[c, h])

        @pl.loop(0, half)
        def _(i):
            b = h * half + i
            a, p = slab[c, b], part[c, b]
            x, y = halo[c, near, b], halo[c, far, b]
            across = jnp.where(near_there, flux(x - a), 0.0)
            own1[c, b] = a + step_size * tv_weight * (flux(p - a) + across)
            near1[c, b] = x + step_size * tv_weight * (flux(y - x) - across)

        send(own1.at[c, some], part1.at[c, some], q_send.at[c], q_recv.at[c, h], partner, me)

    def second_step(c, h):
        wait(part1.at[c, pl.ds(h * half, half)], q_recv.at[c, h])

        @pl.loop(0, half)
        def _(i):
            b = h * half + i
            a, u = slab[c, b], own1[c, b]
            across = jnp.where(near_there, flux(near1[c, b] - u), 0.0)
            result = u - step_size * ((u - a) - tv_weight * (flux(part1[c, b] - u) + across))
            out[0, :, pl.ds(pl.multiple_of(b * width + c * n, n), n)] = result

    @pl.loop(0, chunks)
    def _(c):
        first_step(c, 1 - core)

        @pl.when(c > 0)
        def _():
            second_step(c - 1, core)

        first_step(c, core)
        second_step(c, 1 - core)

    second_step(chunks - 1, core)

    @pl.loop(0, chunks)
    def _(c):
        wait(slab.at[c, pl.ds(0, slabs - 1)], f_send.at[c])
        wait(slab.at[c, pl.ds(0, slabs - 1)], b_send.at[c])
        wait(slab.at[c], p_send.at[c])
        wait(slab.at[c], q_send.at[c])

        @pl.when(full_there)
        def _():
            wait(slab.at[c], h_send.at[c])
            wait(slab.at[c, pl.ds(0, half)], h_send.at[c])

        @pl.when(half_there)
        def _():
            wait(slab.at[c, pl.ds(0, half)], h_send.at[c])


def on_device(volume, measured, cutoff):
    _, rows, pixels = volume.shape
    _, _, length, width = measured.shape
    slabs = pixels // width
    n = 128
    chunks = width // n
    most = 3 * length // 8
    kp = length // 2
    kr = -(-(most + 1) // 16) * 16
    upper = (length - most) // 128 * 128
    kranges = ((0, kp, 0), (upper, length, kp)) if upper >= kp else ((0, length, 0),)
    cfg = (length, slabs, rows, width, n, chunks, kr, kp, kranges)
    piece = (chunks, slabs, rows, n)
    dma = pltpu.SemaphoreType.DMA
    hbm = pl.BlockSpec(memory_space=pl.ANY)
    vmem = pl.BlockSpec(memory_space=pltpu.VMEM)
    return pl.pallas_call(
        functools.partial(kernel, cfg),
        out_shape=pltpu.VMEM(volume.shape, F32),
        in_specs=[hbm, hbm, vmem, hbm, hbm, hbm, hbm],
        out_specs=vmem,
        scratch_shapes=[
            pltpu.VMEM((chunks, length, n), F32),
            pltpu.VMEM((chunks, length, n), F32),
            pltpu.VMEM((chunks, 2, length, n), F32),
            *[pltpu.VMEM((length, length), BF16)] * 4,
            pltpu.VMEM((2, length, 2 * n), BF16),
            pltpu.VMEM((2, kp, 2 * n), BF16),
            pltpu.VMEM(piece, F32),
            pltpu.VMEM((chunks, 2, slabs, rows, n), F32),
            *[pltpu.VMEM(piece, F32)] * 4,
            dma((4,)),
            *[dma((chunks,))] * 5,
            *[dma((chunks,)), dma((chunks, 2))] * 3,
        ],
        compiler_params=pltpu.CompilerParams(
            collective_id=0, has_side_effects=True, vmem_limit_bytes=60 * 1024 * 1024
        ),
        cost_estimate=pl.CostEstimate(flops=10**10, bytes_accessed=2**24, transcendentals=0),
    )(volume, measured, cutoff, *tables(length))


def solution(mesh):
    placed = (P("frame", "slab", None), P("frame", None, None, "slab"), P("frame", "slab"))
    return jax.shard_map(
        on_device, mesh=mesh, in_specs=placed, out_specs=P("frame", "slab", None), check_vma=False
    )
```

```python
import functools

import jax
import jax.numpy as jnp
import ml_dtypes
import numpy as np
from jax import lax
from jax.experimental import pallas as pl
from jax.experimental.pallas import tpu as pltpu
from jax.sharding import PartitionSpec as P

MESH = pl.DeviceIdType.MESH
F32, BF16 = jnp.float32, jnp.bfloat16
step_size = 0.25
tv_weight = 1.0


def tables(length):
    index = np.arange(length, dtype=np.int64)
    angle = (index[:, None] * index[None, :] % length) * (2.0 * np.pi / length)
    parts = []
    for table in (np.cos(angle), -np.sin(angle)):
        table = table / np.sqrt(length)
        head = table.astype(ml_dtypes.bfloat16)
        rest = (table - head.astype(np.float64)).astype(ml_dtypes.bfloat16)
        parts += [head, rest]
    return parts


def flux(d):
    return d * lax.rsqrt(d * d + 1.0)


def split(x):
    head = x.astype(BF16)
    rest = (x - head.astype(F32)).astype(BF16)
    return head, rest


def kernel(
    cfg,
    volume, measured, cutoff, ch_hbm, cl_hbm, sh_hbm, sl_hbm,
    out,
    cols, anchor_cols, meas, ch, cl, sh, sl, rhs, rhs2,
    slab, halo, part, own1, near1, part1,
    local_sem, meas_sem, f_send, f_recv, b_send, b_recv, h_send, h_recv, p_send, p_recv, q_send, q_recv,
):
    length, slabs, rows, width, n, chunks, kr, kp, kranges = cfg
    half = slabs // 2
    ahead = min(2, chunks)
    unroll = min(4, half)
    frame, me = lax.axis_index("frame"), lax.axis_index("slab")
    frames = lax.axis_size("frame")
    block, core = lax.div(frame, 2), lax.rem(frame, 2)
    blocks = frames // 2
    z_lo, place = lax.div(me, half), lax.rem(me, half)
    partner = frame + 1 - 2 * core
    full_frame = jnp.where(z_lo == 1, 2 * block + 2, 2 * block - 1)
    full_there = jnp.where(z_lo == 1, block < blocks - 1, block > 0)
    half_frame = jnp.where(z_lo == 1, 2 * block - 1, 2 * block + 2)
    half_there = jnp.where(z_lo == 1, block > 0, block < blocks - 1)
    near_block = jnp.where(core == 0, block - 1, block + 1)
    near_there = jnp.where(core == 0, block > 0, block < blocks - 1)

    def send(src, dst, send_sem, recv_sem, to_frame, to_slab):
        pltpu.make_async_remote_copy(
            src_ref=src, dst_ref=dst, send_sem=send_sem, recv_sem=recv_sem,
            device_id=(to_frame, to_slab), device_id_type=MESH,
        ).start()

    def wait(like, sem):
        pltpu.make_async_copy(like, like, sem).wait()

    wide = 4 if half == 16 else 1
    deep = half // wide
    x, y = lax.div(place, deep), lax.rem(place, deep)
    ys = [lax.rem(y + j, deep) for j in range(deep)]
    same, other = z_lo * half, (1 - z_lo) * half

    def each_peer(act):
        @pl.loop(0, wide)
        def _(i):
            row = lax.rem(x + i, wide) * deep
            for j in range(deep):
                act(row + ys[j], (i == 0) if j == 0 else False)

    local = [
        pltpu.make_async_copy(src, dst, local_sem.at[i])
        for i, (src, dst) in enumerate(((ch_hbm, ch), (cl_hbm, cl), (sh_hbm, sh), (sl_hbm, sl)))
    ]
    local += [
        pltpu.make_async_copy(measured.at[0, :, :, pl.ds(c * n, n)], meas.at[c], meas_sem.at[c])
        for c in range(chunks)
    ]
    for copy in local:
        copy.start()

    barrier = pltpu.get_barrier_semaphore()

    def greet(to_frame, to_slab):
        pl.semaphore_signal(barrier, inc=1, device_id=(to_frame, to_slab), device_id_type=MESH)

    def unless(own, act):
        if own is False:
            act()
        else:
            pl.when(jnp.logical_not(own))(act)

    def greet_group(at, own):
        greet(frame, other + at)
        unless(own, lambda: greet(frame, same + at))

    def greet_near(at, own):
        greet(2 * near_block, other + at)
        greet(2 * near_block + 1, other + at)

    each_peer(greet_group)

    @pl.when(near_there & (z_lo == core))
    def _():
        each_peer(greet_near)

    greet(partner, me)

    @pl.when(near_there)
    def _():
        greet(2 * near_block, me)
        greet(2 * near_block + 1, me)

    expected = (
        slabs
        + jnp.where(full_there, half + 1, 0)
        + jnp.where(half_there, 1, 0)
    )
    pl.semaphore_wait(barrier, expected)

    def send_columns(c):
        def source(peer):
            return volume.at[0, :, pl.ds(pl.multiple_of(peer * width + c * n, n), n)]

        target = cols.at[c, pl.ds(pl.multiple_of(me * rows, rows), rows), :]

        def give(peer):
            send(source(peer), target, f_send.at[c], f_recv.at[c], frame, peer)

        def both(at, own):
            give(other + at)
            unless(own, lambda: give(same + at))

        each_peer(both)
        pltpu.make_async_copy(source(me), target, f_recv.at[c]).start()

    @pl.loop(0, min(3, chunks))
    def _(c):
        send_columns(c)

    for copy in local[:4]:
        copy.wait()

    if kp > kr:
        rhs2[:, kr:, :] = jnp.zeros((2, kp - kr, 2 * n), BF16)
    tile = min(256, length)
    tiles = length // tile

    def product(at, ranges, right):
        wide, narrow = None, None
        for half_index, (head, rest) in enumerate(((ch, cl), (sh, sl))):
            for low, high, base in ranges:
                both = right[half_index, base : base + high - low, :]
                first = jnp.dot(head[at, low:high], both, preferred_element_type=F32)
                second = jnp.dot(rest[at, low:high], both[:, :n], preferred_element_type=F32)
                wide = first if wide is None else wide + first
                narrow = second if narrow is None else narrow + second
        return wide[:, :n] + wide[:, n:] + narrow

    def limits(c):
        return cutoff[0:1, pl.ds(pl.multiple_of(c * n, n), n)]

    def transform_measured(c):
        limit = limits(c)
        wait(meas.at[c], meas_sem.at[c])
        for low, high, base in kranges:
            k = lax.broadcasted_iota(jnp.int32, (high - low, n), 0) + low
            inside = jnp.minimum(k, length - k) <= limit
            for i in range(2):
                head, rest = split(jnp.where(inside, meas[c, i, low:high, :], 0.0))
                rhs[i, base : base + high - low, :n] = head
                rhs[i, base : base + high - low, n:] = rest

        @pl.loop(0, tiles)
        def _(t):
            at = pl.ds(pl.multiple_of(t * tile, tile), tile)
            anchor_cols[c, at, :] = product(at, kranges, rhs)

    def transform_volume(c):
        wait(cols.at[c], f_recv.at[c])
        head, rest = split(cols[c])
        rhs[0, 0:length, :n] = head
        rhs[0, 0:length, n:] = rest
        k = lax.broadcasted_iota(jnp.int32, (kr, n), 0)
        weight = jnp.where(k <= limits(c), jnp.where(k == 0, 1.0, 2.0), 0.0)
        for i, (head, rest) in enumerate(((ch, cl), (sh, sl))):
            both = rhs[0, 0:length, :]
            wide = jnp.dot(head[:kr, :], both, preferred_element_type=F32)
            narrow = jnp.dot(rest[:kr, :], both[:, :n], preferred_element_type=F32)
            first, second = split((wide[:, :n] + wide[:, n:] + narrow) * weight)
            rhs2[i, :kr, :n] = first
            rhs2[i, :kr, n:] = second

        @pl.loop(0, tiles)
        def _(t):
            at = pl.ds(pl.multiple_of(t * tile, tile), tile)
            anchor_cols[c, at, :] = anchor_cols[c, at, :] + cols[c, at, :] - product(at, ((0, kp, 0),), rhs2)

    def send_back(c):
        def source(peer):
            return anchor_cols.at[c, pl.ds(pl.multiple_of(peer * rows, rows), rows), :]

        def give(peer):
            send(source(peer), slab.at[c, me], b_send.at[c], b_recv.at[c, z_lo], frame, peer)

        def both(at, own):
            give(other + at)
            unless(own, lambda: give(same + at))

        each_peer(both)
        pltpu.make_async_copy(source(me), slab.at[c, me], b_recv.at[c, z_lo]).start()

        @pl.when(full_there)
        def _():
            each_peer(
                lambda at, own: send(
                    source(other + at), halo.at[c, core, me], h_send.at[c], h_recv.at[c, z_lo], full_frame, other + at
                )
            )

    def send_halo(c, h):
        some = pl.ds(h * half, half)
        wait(slab.at[c, some], b_recv.at[c, h])

        @pl.when(full_there)
        def _():
            send(slab.at[c, some], halo.at[c, core, some], h_send.at[c], h_recv.at[c, h], full_frame, me)

        if h is z_lo:

            @pl.when(half_there)
            def _():
                send(slab.at[c, some], halo.at[c, core, some], h_send.at[c], h_recv.at[c, h], half_frame, me)

        send(slab.at[c, some], part.at[c, some], p_send.at[c], p_recv.at[c, h], partner, me)

    @pl.loop(0, ahead)
    def _(c):
        transform_measured(c)

    @pl.loop(0, chunks)
    def _(c):
        transform_volume(c)
        send_back(c)

        @pl.when(c + 3 < chunks)
        def _():
            send_columns(c + 3)

        @pl.when(c + ahead < chunks)
        def _():
            transform_measured(c + ahead)

        @pl.when(c > 0)
        def _():
            send_halo(c - 1, z_lo)
            send_halo(c - 1, 1 - z_lo)

    send_halo(chunks - 1, z_lo)
    send_halo(chunks - 1, 1 - z_lo)

    near, far = 1 - core, core

    def first_step(c, h):
        some = pl.ds(h * half, half)
        wait(part.at[c, some], p_recv.at[c, h])

        @pl.when(near_there)
        def _():
            wait(halo.at[c, 0], h_recv.at[c, h])

        @pl.loop(0, half, unroll=unroll)
        def _(i):
            b = h * half + i
            a = slab[c, b]
            across = jnp.where(near_there, flux(halo[c, near, b] - a), 0.0)
            own1[c, b] = a + step_size * tv_weight * (flux(part[c, b] - a) + across)
            near1[c, b] = across

        send(own1.at[c, some], part1.at[c, some], q_send.at[c], q_recv.at[c, h], partner, me)

        @pl.loop(0, half, unroll=unroll)
        def _(i):
            b = h * half + i
            x = halo[c, near, b]
            near1[c, b] = x + step_size * tv_weight * (flux(halo[c, far, b] - x) - near1[c, b])

    def second_step(c, h):
        wait(part1.at[c, pl.ds(h * half, half)], q_recv.at[c, h])

        @pl.loop(0, half, unroll=unroll)
        def _(i):
            b = h * half + i
            a, u = slab[c, b], own1[c, b]
            across = jnp.where(near_there, flux(near1[c, b] - u), 0.0)
            result = u - step_size * ((u - a) - tv_weight * (flux(part1[c, b] - u) + across))
            out[0, :, pl.ds(pl.multiple_of(b * width + c * n, n), n)] = result

    @pl.loop(0, chunks)
    def _(c):
        first_step(c, 1 - core)

        @pl.when(c > 0)
        def _():
            second_step(c - 1, core)

        first_step(c, core)
        second_step(c, 1 - core)

    second_step(chunks - 1, core)

    @pl.loop(0, chunks)
    def _(c):
        wait(slab.at[c, pl.ds(0, slabs - 1)], f_send.at[c])
        wait(slab.at[c, pl.ds(0, slabs - 1)], b_send.at[c])
        wait(slab.at[c], p_send.at[c])
        wait(slab.at[c], q_send.at[c])

        @pl.when(full_there)
        def _():
            wait(slab.at[c], h_send.at[c])
            wait(slab.at[c, pl.ds(0, half)], h_send.at[c])

        @pl.when(half_there)
        def _():
            wait(slab.at[c, pl.ds(0, half)], h_send.at[c])


def on_device(volume, measured, cutoff):
    _, rows, pixels = volume.shape
    _, _, length, width = measured.shape
    slabs = pixels // width
    n = 128
    chunks = width // n
    most = 3 * length // 8
    kp = length // 2
    kr = -(-(most + 1) // 16) * 16
    upper = (length - most) // 128 * 128
    kranges = ((0, kp, 0), (upper, length, kp)) if upper >= kp else ((0, length, 0),)
    cfg = (length, slabs, rows, width, n, chunks, kr, kp, kranges)
    piece = (chunks, slabs, rows, n)
    dma = pltpu.SemaphoreType.DMA
    hbm = pl.BlockSpec(memory_space=pl.ANY)
    vmem = pl.BlockSpec(memory_space=pltpu.VMEM)
    return pl.pallas_call(
        functools.partial(kernel, cfg),
        out_shape=pltpu.VMEM(volume.shape, F32),
        in_specs=[hbm, hbm, vmem, hbm, hbm, hbm, hbm],
        out_specs=vmem,
        scratch_shapes=[
            pltpu.VMEM((chunks, length, n), F32),
            pltpu.VMEM((chunks, length, n), F32),
            pltpu.VMEM((chunks, 2, length, n), F32),
            *[pltpu.VMEM((length, length), BF16)] * 4,
            pltpu.VMEM((2, length, 2 * n), BF16),
            pltpu.VMEM((2, kp, 2 * n), BF16),
            pltpu.VMEM(piece, F32),
            pltpu.VMEM((chunks, 2, slabs, rows, n), F32),
            *[pltpu.VMEM(piece, F32)] * 4,
            dma((4,)),
            *[dma((chunks,))] * 3,
            *[dma((chunks,)), dma((chunks, 2))] * 4,
        ],
        compiler_params=pltpu.CompilerParams(
            collective_id=0, has_side_effects=True, vmem_limit_bytes=60 * 1024 * 1024
        ),
        cost_estimate=pl.CostEstimate(flops=10**10, bytes_accessed=2**24, transcendentals=0),
    )(volume, measured, cutoff, *tables(length))


def solution(mesh):
    placed = (P("frame", "slab", None), P("frame", None, None, "slab"), P("frame", "slab"))
    return jax.shard_map(
        on_device, mesh=mesh, in_specs=placed, out_specs=P("frame", "slab", None), check_vma=False
    )
```

```python
import functools

import jax
import jax.numpy as jnp
import ml_dtypes
import numpy as np
from jax import lax
from jax.experimental import pallas as pl
from jax.experimental.pallas import tpu as pltpu
from jax.sharding import PartitionSpec as P

MESH = pl.DeviceIdType.MESH
F32, BF16 = jnp.float32, jnp.bfloat16
step_size = 0.25
tv_weight = 1.0


def tables(length):
    index = np.arange(length, dtype=np.int64)
    angle = (index[:, None] * index[None, :] % length) * (2.0 * np.pi / length)
    parts = []
    for table in (np.cos(angle), -np.sin(angle)):
        table = table / np.sqrt(length)
        head = table.astype(ml_dtypes.bfloat16)
        rest = (table - head.astype(np.float64)).astype(ml_dtypes.bfloat16)
        parts += [head, rest]
    return parts


def flux(d):
    return d * lax.rsqrt(d * d + 1.0)


def split(x):
    head = x.astype(BF16)
    rest = (x - head.astype(F32)).astype(BF16)
    return head, rest


def kernel(
    cfg,
    volume, measured, cutoff, ch_hbm, cl_hbm, sh_hbm, sl_hbm,
    out,
    cols, anchor_cols, meas, ch, cl, sh, sl, rhs, rhs2,
    slab, halo, part, own1, near1, part1,
    local_sem, meas_sem, f_send, f_recv, b_send, b_recv, h_send, h_recv, p_send, p_recv, q_send, q_recv,
):
    length, slabs, rows, width, n, chunks, kr, kp, kranges = cfg
    half = slabs // 2
    ahead = min(2, chunks)
    unroll = min(4, half)
    frame, me = lax.axis_index("frame"), lax.axis_index("slab")
    frames = lax.axis_size("frame")
    block, core = lax.div(frame, 2), lax.rem(frame, 2)
    blocks = frames // 2
    z_lo, place = lax.div(me, half), lax.rem(me, half)
    partner = frame + 1 - 2 * core
    full_frame = jnp.where(z_lo == 1, 2 * block + 2, 2 * block - 1)
    full_there = jnp.where(z_lo == 1, block < blocks - 1, block > 0)
    half_frame = jnp.where(z_lo == 1, 2 * block - 1, 2 * block + 2)
    half_there = jnp.where(z_lo == 1, block > 0, block < blocks - 1)
    near_block = jnp.where(core == 0, block - 1, block + 1)
    near_there = jnp.where(core == 0, block > 0, block < blocks - 1)

    def send(src, dst, send_sem, recv_sem, to_frame, to_slab):
        pltpu.make_async_remote_copy(
            src_ref=src, dst_ref=dst, send_sem=send_sem, recv_sem=recv_sem,
            device_id=(to_frame, to_slab), device_id_type=MESH,
        ).start()

    def wait(like, sem):
        pltpu.make_async_copy(like, like, sem).wait()

    wide = 4 if half == 16 else 1
    deep = half // wide
    x, y = lax.div(place, deep), lax.rem(place, deep)
    ys = [lax.rem(y + j, deep) for j in range(deep)]
    same, other = z_lo * half, (1 - z_lo) * half

    def each_peer(act):
        @pl.loop(0, wide)
        def _(i):
            row = lax.rem(x + i, wide) * deep
            for j in range(deep):
                act(row + ys[j], (i == 0) if j == 0 else False)

    local = [
        pltpu.make_async_copy(src, dst, local_sem.at[i])
        for i, (src, dst) in enumerate(((ch_hbm, ch), (cl_hbm, cl), (sh_hbm, sh), (sl_hbm, sl)))
    ]
    local += [
        pltpu.make_async_copy(measured.at[0, :, :, pl.ds(c * n, n)], meas.at[c], meas_sem.at[c])
        for c in range(chunks)
    ]
    for copy in local:
        copy.start()

    barrier = pltpu.get_barrier_semaphore()

    def greet(to_frame, to_slab):
        pl.semaphore_signal(barrier, inc=1, device_id=(to_frame, to_slab), device_id_type=MESH)

    def unless(own, act):
        if own is False:
            act()
        else:
            pl.when(jnp.logical_not(own))(act)

    def greet_group(at, own):
        greet(frame, other + at)
        unless(own, lambda: greet(frame, same + at))

    def greet_near(at, own):
        greet(2 * near_block, other + at)
        greet(2 * near_block + 1, other + at)

    each_peer(greet_group)

    @pl.when(near_there & (z_lo == core))
    def _():
        each_peer(greet_near)

    greet(partner, me)

    @pl.when(near_there)
    def _():
        greet(2 * near_block, me)
        greet(2 * near_block + 1, me)

    expected = (
        slabs
        + jnp.where(full_there, half + 1, 0)
        + jnp.where(half_there, 1, 0)
    )
    pl.semaphore_wait(barrier, expected)

    def send_columns(c):
        def source(peer):
            return volume.at[0, :, pl.ds(pl.multiple_of(peer * width + c * n, n), n)]

        target = cols.at[c, pl.ds(pl.multiple_of(me * rows, rows), rows), :]

        def give(peer):
            send(source(peer), target, f_send.at[c], f_recv.at[c], frame, peer)

        def both(at, own):
            give(other + at)
            unless(own, lambda: give(same + at))

        each_peer(both)
        pltpu.make_async_copy(source(me), target, f_recv.at[c]).start()

    @pl.loop(0, min(3, chunks))
    def _(c):
        send_columns(c)

    for copy in local[:4]:
        copy.wait()

    if kp > kr:
        rhs2[:, kr:, :] = jnp.zeros((2, kp - kr, 2 * n), BF16)
    tile = min(256, length)
    tiles = length // tile

    def product(at, ranges, right):
        wide, narrow = None, None
        for half_index, (head, rest) in enumerate(((ch, cl), (sh, sl))):
            for low, high, base in ranges:
                both = right[half_index, base : base + high - low, :]
                first = jnp.dot(head[at, low:high], both, preferred_element_type=F32)
                second = jnp.dot(rest[at, low:high], both[:, :n], preferred_element_type=F32)
                wide = first if wide is None else wide + first
                narrow = second if narrow is None else narrow + second
        return wide[:, :n] + wide[:, n:] + narrow

    edge = (block == 0) | (block == blocks - 1)

    def limits(c):
        return cutoff[0:1, pl.ds(pl.multiple_of(c * n, n), n)]

    def transform_measured(c):
        limit = limits(c)
        wait(meas.at[c], meas_sem.at[c])
        for low, high, base in kranges:
            k = lax.broadcasted_iota(jnp.int32, (high - low, n), 0) + low
            inside = jnp.minimum(k, length - k) <= limit
            for i in range(2):
                head, rest = split(jnp.where(inside, meas[c, i, low:high, :], 0.0))
                rhs[i, base : base + high - low, :n] = head
                rhs[i, base : base + high - low, n:] = rest

        @pl.loop(0, tiles)
        def _(t):
            at = pl.ds(pl.multiple_of(t * tile, tile), tile)
            anchor_cols[c, at, :] = product(at, kranges, rhs)

    def transform_volume(c):
        wait(cols.at[c], f_recv.at[c])
        head, rest = split(cols[c])
        rhs[0, 0:length, :n] = head
        rhs[0, 0:length, n:] = rest
        k = lax.broadcasted_iota(jnp.int32, (kr, n), 0)
        weight = jnp.where(k <= limits(c), jnp.where(k == 0, 1.0, 2.0), 0.0)
        for i, (head, rest) in enumerate(((ch, cl), (sh, sl))):
            both = rhs[0, 0:length, :]
            wide = jnp.dot(head[:kr, :], both, preferred_element_type=F32)
            narrow = jnp.dot(rest[:kr, :], both[:, :n], preferred_element_type=F32)
            first, second = split((wide[:, :n] + wide[:, n:] + narrow) * weight)
            rhs2[i, :kr, :n] = first
            rhs2[i, :kr, n:] = second

        @pl.loop(0, tiles)
        def _(t):
            at = pl.ds(pl.multiple_of(t * tile, tile), tile)
            anchor_cols[c, at, :] = anchor_cols[c, at, :] + cols[c, at, :] - product(at, ((0, kp, 0),), rhs2)

    def send_back(c):
        def source(peer):
            return anchor_cols.at[c, pl.ds(pl.multiple_of(peer * rows, rows), rows), :]

        def give(peer):
            send(source(peer), slab.at[c, me], b_send.at[c], b_recv.at[c, z_lo], frame, peer)

        def both(at, own):
            give(other + at)
            unless(own, lambda: give(same + at))

        each_peer(both)
        pltpu.make_async_copy(source(me), slab.at[c, me], b_recv.at[c, z_lo]).start()

        @pl.when(full_there)
        def _():
            each_peer(
                lambda at, own: send(
                    source(other + at), halo.at[c, core, me], h_send.at[c], h_recv.at[c, z_lo], full_frame, other + at
                )
            )

    def send_halo(c, h):
        some = pl.ds(h * half, half)
        wait(slab.at[c, some], b_recv.at[c, h])

        @pl.when(full_there)
        def _():
            send(slab.at[c, some], halo.at[c, core, some], h_send.at[c], h_recv.at[c, h], full_frame, me)

        if h is z_lo:

            @pl.when(half_there)
            def _():
                send(slab.at[c, some], halo.at[c, core, some], h_send.at[c], h_recv.at[c, h], half_frame, me)

        send(slab.at[c, some], part.at[c, some], p_send.at[c], p_recv.at[c, h], partner, me)

    @pl.loop(0, ahead)
    def _(c):
        transform_measured(c)

    @pl.loop(0, chunks)
    def _(c):
        transform_volume(c)
        send_back(c)

        @pl.when(c + 3 < chunks)
        def _():
            send_columns(c + 3)

        @pl.when(c + ahead < chunks)
        def _():
            transform_measured(c + ahead)

        late = jnp.where(edge, 0, 1)

        @pl.when(c >= late)
        def _():
            send_halo(c - late, z_lo)
            send_halo(c - late, 1 - z_lo)

    @pl.when(jnp.logical_not(edge))
    def _():
        send_halo(chunks - 1, z_lo)
        send_halo(chunks - 1, 1 - z_lo)

    near, far = 1 - core, core

    def first_step(c, h):
        some = pl.ds(h * half, half)
        wait(part.at[c, some], p_recv.at[c, h])

        @pl.when(near_there)
        def _():
            wait(halo.at[c, 0], h_recv.at[c, h])

        @pl.loop(0, half, unroll=unroll)
        def _(i):
            b = h * half + i
            a = slab[c, b]
            across = jnp.where(near_there, flux(halo[c, near, b] - a), 0.0)
            own1[c, b] = a + step_size * tv_weight * (flux(part[c, b] - a) + across)
            near1[c, b] = across

        send(own1.at[c, some], part1.at[c, some], q_send.at[c], q_recv.at[c, h], partner, me)

        @pl.loop(0, half, unroll=unroll)
        def _(i):
            b = h * half + i
            x = halo[c, near, b]
            near1[c, b] = x + step_size * tv_weight * (flux(halo[c, far, b] - x) - near1[c, b])

    def second_step(c, h):
        wait(part1.at[c, pl.ds(h * half, half)], q_recv.at[c, h])

        @pl.loop(0, half, unroll=unroll)
        def _(i):
            b = h * half + i
            a, u = slab[c, b], own1[c, b]
            across = jnp.where(near_there, flux(near1[c, b] - u), 0.0)
            result = u - step_size * ((u - a) - tv_weight * (flux(part1[c, b] - u) + across))
            out[0, :, pl.ds(pl.multiple_of(b * width + c * n, n), n)] = result

    @pl.loop(0, chunks)
    def _(c):
        first_step(c, 1 - core)

        @pl.when(c > 0)
        def _():
            second_step(c - 1, core)

        first_step(c, core)
        second_step(c, 1 - core)

    second_step(chunks - 1, core)

    @pl.loop(0, chunks)
    def _(c):
        wait(slab.at[c, pl.ds(0, slabs - 1)], f_send.at[c])
        wait(slab.at[c, pl.ds(0, slabs - 1)], b_send.at[c])
        wait(slab.at[c], p_send.at[c])
        wait(slab.at[c], q_send.at[c])

        @pl.when(full_there)
        def _():
            wait(slab.at[c], h_send.at[c])
            wait(slab.at[c, pl.ds(0, half)], h_send.at[c])

        @pl.when(half_there)
        def _():
            wait(slab.at[c, pl.ds(0, half)], h_send.at[c])


def on_device(volume, measured, cutoff):
    _, rows, pixels = volume.shape
    _, _, length, width = measured.shape
    slabs = pixels // width
    n = 128
    chunks = width // n
    most = 3 * length // 8
    kp = length // 2
    kr = -(-(most + 1) // 16) * 16
    upper = (length - most) // 128 * 128
    kranges = ((0, kp, 0), (upper, length, kp)) if upper >= kp else ((0, length, 0),)
    cfg = (length, slabs, rows, width, n, chunks, kr, kp, kranges)
    piece = (chunks, slabs, rows, n)
    dma = pltpu.SemaphoreType.DMA
    hbm = pl.BlockSpec(memory_space=pl.ANY)
    vmem = pl.BlockSpec(memory_space=pltpu.VMEM)
    return pl.pallas_call(
        functools.partial(kernel, cfg),
        out_shape=pltpu.VMEM(volume.shape, F32),
        in_specs=[hbm, hbm, vmem, hbm, hbm, hbm, hbm],
        out_specs=vmem,
        scratch_shapes=[
            pltpu.VMEM((chunks, length, n), F32),
            pltpu.VMEM((chunks, length, n), F32),
            pltpu.VMEM((chunks, 2, length, n), F32),
            *[pltpu.VMEM((length, length), BF16)] * 4,
            pltpu.VMEM((2, length, 2 * n), BF16),
            pltpu.VMEM((2, kp, 2 * n), BF16),
            pltpu.VMEM(piece, F32),
            pltpu.VMEM((chunks, 2, slabs, rows, n), F32),
            *[pltpu.VMEM(piece, F32)] * 4,
            dma((4,)),
            *[dma((chunks,))] * 3,
            *[dma((chunks,)), dma((chunks, 2))] * 4,
        ],
        compiler_params=pltpu.CompilerParams(
            collective_id=0, has_side_effects=True, vmem_limit_bytes=60 * 1024 * 1024
        ),
        cost_estimate=pl.CostEstimate(flops=10**10, bytes_accessed=2**24, transcendentals=0),
    )(volume, measured, cutoff, *tables(length))


def solution(mesh):
    placed = (P("frame", "slab", None), P("frame", None, None, "slab"), P("frame", "slab"))
    return jax.shard_map(
        on_device, mesh=mesh, in_specs=placed, out_specs=P("frame", "slab", None), check_vma=False
    )
```
